32 devices in a mesh: region: 2 (over y), visit: 8 (over z, x), tile: 2 (over core).
Axes of the slice: x: 2, y: 2, z: 4, core: 2. Of those that a mesh axis runs over, the one named last changes fastest.
Arguments:
- science: bfloat16 [16, 8, 32, 512], P(('region', 'visit'), None, None, 'tile'), parts along dimension 0, may hold values from -6 to 6
- warped: bfloat16 [16, 8, 32, 512], P(('region', 'visit'), None, None, 'tile'), parts along dimension 0, may hold values from -6 to 6
- weights: float32 [16], P('region'), parts along dimension 0, may hold values from 0.2 to 5
- coef: float32 [16, 8, 13, 6], P(('region', 'visit')), parts along dimension 0, may hold values from -3 to 3
- basis_rows: bfloat16 [13, 17], replicated, may hold values from -1.5 to 1.5
- basis_cols: bfloat16 [13, 17], replicated, may hold values from -1.5 to 1.5
- covered: int32 [16, 8], P('region'), parts along dimension 0, may hold values from 0 to 7, all different within a row
- owner: int32 [16], P('region'), parts along dimension 0, may hold values from 0 to 7, each once
Outputs:
- templates: bfloat16 [16, 32, 512], P(('region', 'visit'), None, 'tile'), parts along dimension 0
- difference: float32 [16, 8, 32, 512], P(('region', 'visit'), None, None, 'tile'), parts along dimension 0
The draws below stay inside these ranges and needn't reach their ends.
There are 2 independent parts, one for each index of `region`. The reference program is written for one: setup_inputs(seed, part) draws one part's arguments, and reference() takes and returns one part's arrays. A program takes and returns all parts, laid end to end along the dimension named above; an argument that names none is the same for every part. Nothing has to cross between parts.
Inputs may be any that keep to these rules, and one draw needn't show every extreme that they name: `covered`: each row names 8 different tiles, and every tile is named by some row. `owner`: each slot once.
All inputs are finite; a program needn't handle non-finite values.
Results may differ from the reference program's by a relative error of at most 0.0022.
Values may be sent and summed in bfloat16 or wider, within the bound.
A program may use at most 64 MiB of HBM per device.

```python
import math
import jax
import jax.numpy as jnp
from jax import lax

ROWS = 32
COLS = 512
BASIS = 13
KSIZE = 17
TERMS = 6
TILES = 8
VISITS = 8
COVER = 8


def block_levels(rng, extent, cuts, low, high):
    loudness = 1.0
    for dim, parts in cuts:
        draws = jax.random.uniform(jax.random.fold_in(jax.random.fold_in(rng, 6), dim), (parts,), jnp.float32, low / len(cuts), high / len(cuts))
        loudness = loudness * jnp.repeat(jnp.exp(draws), extent[dim] // parts).reshape((-1,) + (1,) * (len(extent) - 1 - dim))
    return loudness


def different_ones(rng, rows, number_of, top, lift):
    ranking = jax.random.permutation(jax.random.fold_in(rng, 1), number_of)
    boost = ranking
    for power in range(3):
        boost = boost * boost // number_of
    boost = boost * lift // number_of
    chance = jax.random.randint(jax.random.fold_in(rng, 2), (rows, number_of), 0, 4096) + boost
    sure = jax.random.permutation(jax.random.fold_in(rng, 3), rows)[jnp.arange(number_of) % rows]
    chance = jnp.where(jnp.arange(rows)[:, None] == sure[None, :], 1 << 14, chance)
    merit = chance * number_of + jnp.arange(number_of)
    return lax.top_k(merit.astype(jnp.int32), top)[1].astype(jnp.int32)


def gaussian(stream_key, shape, scale, most, shards=(), held_as=jnp.bfloat16):
    factor_of = block_levels(stream_key, shape, shards, -0.22, 0.18) if shards else 1.0
    values = jax.random.normal(stream_key, shape, jnp.float32) * scale * factor_of
    return jnp.minimum(jnp.maximum(values, -most), most).astype(held_as)


def setup_inputs(seed: int = 0, part: int = 0) -> dict:
    arg_keys = jax.random.split(jax.random.key(seed), 9)
    part_keys = jax.random.split(jax.random.fold_in(arg_keys[8], part), 9)
    return {
        "science": gaussian(part_keys[0], (VISITS, COVER, ROWS, COLS), 1.0, 6.0, ((0, 8), (3, 2))),
        "warped": gaussian(part_keys[1], (VISITS, COVER, ROWS, COLS), 1.0, 6.0, ((0, 8), (3, 2))),
        "weights": jnp.clip(jnp.exp(jax.random.uniform(part_keys[2], (VISITS,), jnp.float32, math.log(0.2), math.log(5.0))), 0.2, 5.0),
        "coef": gaussian(part_keys[3], (VISITS, COVER, BASIS, TERMS), 0.5, 3.0, ((0, 8),), jnp.float32),
        "basis_rows": gaussian(arg_keys[4], (BASIS, KSIZE), KSIZE ** -0.5, 1.5),
        "basis_cols": gaussian(arg_keys[5], (BASIS, KSIZE), KSIZE ** -0.5, 1.5),
        "covered": different_ones(part_keys[6], VISITS, TILES, COVER, 8192),
        "owner": jax.random.permutation(part_keys[7], TILES).astype(jnp.int32),
    }


def polynomials(rows, cols):
    yn = (2.0 * jnp.arange(rows, dtype=jnp.float32) + 1.0) / rows - 1.0
    xn = (2.0 * jnp.arange(cols, dtype=jnp.float32) + 1.0) / cols - 1.0
    ygrid = jnp.broadcast_to(yn[:, None], (rows, cols))
    xgrid = jnp.broadcast_to(xn[None, :], (rows, cols))
    ones = jnp.ones((rows, cols), jnp.float32)
    return jnp.stack([ones, xgrid, ygrid, xgrid * xgrid, xgrid * ygrid, ygrid * ygrid])


def reference(science, warped, weights, coef, basis_rows, basis_cols, covered, owner):
    reach = KSIZE // 2

    def add_visit(acc, item):
        over, image, weight = item
        return acc.at[over].add(weight * image.astype(jnp.float32)), None

    sums, unused = lax.scan(add_visit, jnp.zeros((TILES, ROWS, COLS), jnp.float32), (covered, warped, weights))
    weight_sum = jnp.zeros((TILES,), jnp.float32).at[covered.reshape(-1)].add(jnp.repeat(weights, COVER))
    coadd = (sums / weight_sum[:, None, None]).astype(jnp.bfloat16)
    templates = jnp.zeros_like(coadd).at[owner].set(coadd)
    polys = polynomials(ROWS, COLS)
    rows_f = basis_rows.astype(jnp.float32)
    cols_f = basis_cols.astype(jnp.float32)

    def per_visit(item):
        sci, over, cf = item
        tpl = jnp.take(coadd, over, axis=0).astype(jnp.float32)
        padded = jnp.pad(tpl, ((0, 0), (reach, reach), (0, 0)))
        blurred = jnp.zeros((COVER, BASIS, ROWS, COLS), jnp.float32)
        for i in range(KSIZE):
            blurred = blurred + rows_f[None, :, i, None, None] * padded[:, None, i:i + ROWS, :]
        blurred = lax.optimization_barrier(blurred.astype(jnp.bfloat16)).astype(jnp.float32)
        padded = jnp.pad(blurred, ((0, 0), (0, 0), (0, 0), (reach, reach)))
        smooth = jnp.zeros((COVER, BASIS, ROWS, COLS), jnp.float32)
        for j in range(KSIZE):
            smooth = smooth + cols_f[None, :, j, None, None] * padded[:, :, :, j:j + COLS]
        factor = jnp.einsum('kbp,pyx->kbyx', cf, polys, precision=lax.Precision.HIGHEST)
        return sci.astype(jnp.float32) - jnp.sum(factor * smooth, axis=1)

    difference = lax.map(per_visit, (science, covered, coef))
    return templates, difference
```

```python
import functools

import jax
import jax.numpy as jnp
from jax import lax
from jax.experimental import pallas as pl
from jax.experimental.pallas import tpu as pltpu
from jax.sharding import PartitionSpec as P

MESH = pl.DeviceIdType.MESH
LANES = 128


def padded(block, sides, width):
    for axis, dim in sides:
        count = lax.axis_size(axis)
        forward = [(i, i + 1) for i in range(count - 1)]
        backward = [(target, source) for source, target in forward]
        low = lax.ppermute(
            lax.slice_in_dim(block, block.shape[dim] - width, None, axis=dim), axis, forward
        )
        high = lax.ppermute(lax.slice_in_dim(block, 0, width, axis=dim), axis, backward)
        block = jnp.concatenate([low, block, high], axis=dim)
    return block


def polynomials(rows, half, offset, total):
    yn = (2.0 * jnp.arange(rows, dtype=jnp.float32) + 1.0) / rows - 1.0
    columns = (offset + lax.iota(jnp.int32, half)).astype(jnp.float32)
    xn = (2.0 * columns + 1.0) / total - 1.0
    ygrid = jnp.broadcast_to(yn[:, None], (rows, half))
    xgrid = jnp.broadcast_to(xn[None, :], (rows, half))
    ones = jnp.ones((rows, half), jnp.float32)
    return jnp.stack([ones, xgrid, ygrid, xgrid * xgrid, xgrid * ygrid, ygrid * ygrid])


def band_matrix(profile, offsets):
    band = jnp.zeros((profile.shape[0],) + offsets.shape, jnp.bfloat16)
    for i in range(profile.shape[1]):
        band = jnp.where((offsets == i)[None], profile[:, i][:, None, None], band)
    return band


def sparse_body(science, warped, weights, coef, basis_rows, basis_cols, covered, owner):
    count, rows, half = (warped.shape[1], warped.shape[2], warped.shape[3])
    tiles = owner.shape[0]
    visit_count = lax.axis_size("visit")
    visit_here = lax.axis_index("visit")
    side_here = lax.axis_index("tile")
    side_count = lax.axis_size("tile")
    tile_dev = tiles // visit_count
    ksize = basis_rows.shape[1]
    reach = ksize // 2
    width = half + 2 * reach
    wanted = lax.iota(jnp.int32, tiles)
    slots = jnp.take(owner, covered)
    slot_of = lax.dynamic_slice_in_dim(slots, visit_here, 1, 0)[0]
    hits = (slots[:, :, None] == wanted).astype(jnp.float32)
    slot_weight = jnp.sum(weights[:, None, None] * hits, axis=(0, 1))
    flat_pixels = warped[0].reshape(count, rows * half)
    select = (slot_of[None, :] == wanted[:, None]).astype(jnp.bfloat16)
    packed = jnp.dot(select, flat_pixels, preferred_element_type=jnp.float32).astype(jnp.bfloat16)
    received = lax.all_to_all(packed, "visit", split_axis=0, concat_axis=0, tiled=True)
    received = received.reshape(visit_count, tile_dev, rows * half)
    total = jnp.sum(weights[:, None, None] * received.astype(jnp.float32), axis=0)
    mine_weight = lax.dynamic_slice_in_dim(slot_weight, visit_here * tile_dev, tile_dev, 0)
    templates = (total / mine_weight[:, None]).astype(jnp.bfloat16).reshape(tile_dev, rows, half)
    library = lax.all_gather(templates, "visit", axis=0, tiled=True)
    chosen = jnp.take(library, slot_of, axis=0)
    chosen = padded(chosen, (("tile", 2),), reach)
    row_offsets = lax.iota(jnp.int32, rows)[None, :] - lax.iota(jnp.int32, rows)[:, None] + reach
    row_band = band_matrix(basis_rows, row_offsets)
    col_offsets = lax.iota(jnp.int32, width)[:, None] - lax.iota(jnp.int32, half)[None, :]
    col_band = band_matrix(basis_cols, col_offsets)
    polys = polynomials(rows, half, side_here * half, half * side_count)
    pairs = count // 2
    tpl_blocks = chosen.reshape(pairs, 2, rows, width)
    sci_blocks = science[0].reshape(pairs, 2, rows, half)
    coef_blocks = coef[0].reshape(pairs, 2, coef.shape[2], coef.shape[3])

    def match(item):
        tpl, sci, cf = item
        blurred = jnp.einsum(
            "byz,kzx->kbyx", row_band, tpl, preferred_element_type=jnp.float32
        ).astype(jnp.bfloat16)
        smooth = jnp.einsum("kbyx,bxw->kbyw", blurred, col_band, preferred_element_type=jnp.float32)
        factor = jnp.einsum("kbp,pyw->kbyw", cf, polys, precision=lax.Precision.HIGHEST)
        return sci.astype(jnp.float32) - jnp.sum(factor * smooth, axis=1)

    difference = lax.map(match, (tpl_blocks, sci_blocks, coef_blocks)).reshape(1, count, rows, half)
    return (templates, difference)


def match_kernel(
    n,
    warped_hbm,
    coef_ref,
    rows_ref,
    cols_ref,
    weights_ref,
    covered_ref,
    owner_ref,
    templates_ref,
    model_ref,
    warped,
    packed,
    received,
    library,
    edges,
    chosen,
    profiles,
    row_band,
    col_band,
    factor,
    blurred,
    load_sem,
    send1,
    recv1,
    send2,
    recv2,
    send3,
    recv3,
):
    count, rows, half = warped.shape
    basis, ksize = rows_ref.shape
    reach = ksize // 2
    me = lax.axis_index("visit")
    side = lax.axis_index("tile")
    group = LANES // rows
    groups = count // group

    load = pltpu.make_async_copy(warped_hbm.at[0], warped, load_sem)
    load.start()
    barrier = pltpu.get_barrier_semaphore()
    for d in range(1, n):
        pl.semaphore_signal(
            barrier, inc=1, device_id={"visit": lax.rem(me + d, n)}, device_id_type=MESH
        )
    pl.semaphore_signal(barrier, inc=1, device_id={"tile": 1 - side}, device_id_type=MESH)

    slots = [owner_ref[covered_ref[me, k]] for k in range(count)]
    load.wait()
    for d in range(n):
        target = lax.rem(me + d, n)
        k_of = jnp.int32(0)
        for k in range(1, count):
            k_of = jnp.where(slots[k] == target, jnp.int32(k), k_of)
        packed[d] = warped[k_of]
    pl.semaphore_wait(barrier, n)

    exchange = []
    for d in range(1, n):
        exchange.append(
            pltpu.make_async_remote_copy(
                src_ref=packed.at[d],
                dst_ref=received.at[d],
                send_sem=send1.at[d],
                recv_sem=recv1.at[d],
                device_id={"visit": lax.rem(me + d, n)},
                device_id_type=MESH,
            )
        )
        exchange[-1].start()

    profiles[...] = jnp.zeros_like(profiles)
    profiles[0, 0:basis, 0:ksize] = rows_ref[...].astype(jnp.float32)
    profiles[1, 0:basis, 0:ksize] = cols_ref[...].astype(jnp.float32)
    zi = lax.broadcasted_iota(jnp.int32, (LANES, LANES), 0)
    xi = lax.broadcasted_iota(jnp.int32, (LANES, LANES), 1)
    flip = (zi + xi == ksize - 1).astype(jnp.bfloat16)
    profiles[1] = jnp.dot(
        profiles[1].astype(jnp.bfloat16), flip, preferred_element_type=jnp.float32
    )
    same = (zi // rows) == (xi // rows)
    centre = jnp.abs(zi - xi) <= reach
    above = zi - xi > LANES // 2
    below = xi - zi > LANES // 2
    zero = jnp.zeros((LANES, LANES), jnp.float32)

    def circulant(which, b):
        line = jnp.broadcast_to(profiles[which, b : b + 1, :], (LANES, LANES))
        return pltpu.roll(line, LANES - reach, 1, stride=1, stride_axis=0)

    for b in range(basis):
        row_band[b * LANES : (b + 1) * LANES, :] = jnp.where(same, circulant(0, b), zero).astype(
            jnp.bfloat16
        )
        ring = circulant(1, b)
        diagonal = jnp.where(centre, ring, zero).astype(jnp.bfloat16)
        upper = jnp.where(above, ring, zero)
        lower = jnp.where(below, ring, zero)
        for j in range(half // LANES):
            for i in range(half // LANES):
                block = (
                    diagonal
                    if i == j
                    else upper.astype(jnp.bfloat16)
                    if i == j - 1
                    else lower.astype(jnp.bfloat16)
                    if i == j + 1
                    else zero.astype(jnp.bfloat16)
                )
                col_band[b, i * LANES : (i + 1) * LANES, j * LANES : (j + 1) * LANES] = block
            edge = zero
            if j == half // LANES - 1:
                edge = jnp.where(side == 0, lower, edge)
            if j == 0:
                edge = jnp.where(side == 1, upper, edge)
            col_band[b, half : half + LANES, j * LANES : (j + 1) * LANES] = edge.astype(
                jnp.bfloat16
            )

    terms = coef_ref.shape[3]
    line = lax.broadcasted_iota(jnp.int32, (3 * rows, terms), 0)
    term = lax.broadcasted_iota(jnp.int32, (3 * rows, terms), 1)
    power = line // rows
    yn = (2.0 * (line % rows).astype(jnp.float32) + 1.0) / rows - 1.0
    one = jnp.ones_like(yn)
    none = jnp.zeros_like(yn)
    constant = jnp.where(term == 0, one, jnp.where(term == 2, yn, jnp.where(term == 5, yn * yn, none)))
    linear = jnp.where(term == 1, one, jnp.where(term == 4, yn, none))
    square = jnp.where(term == 3, one, none)
    vertical = jnp.where(power == 0, constant, jnp.where(power == 1, linear, square))
    column = lax.broadcasted_iota(jnp.int32, (rows, half), 1) + side * half
    xn = (2.0 * column.astype(jnp.float32) + 1.0) / (2 * half) - 1.0

    def factors(k, carry):
        parts = lax.dot_general(
            vertical,
            coef_ref[0, k],
            (((1,), (1,)), ((), ())),
            precision=lax.Precision.HIGHEST,
            preferred_element_type=jnp.float32,
        )
        start = pl.multiple_of(k * rows, rows)
        for b in range(basis):
            p0 = parts[0:rows, b : b + 1]
            p1 = parts[rows : 2 * rows, b : b + 1]
            p2 = parts[2 * rows : 3 * rows, b : b + 1]
            factor[b, pl.ds(start, rows), :] = p0 + xn * (p1 + xn * p2)
        return carry

    lax.fori_loop(0, count, factors, 0)

    weight_sum = weights_ref[0]
    for v in range(1, n):
        weight_sum = weight_sum + weights_ref[v]
    total = weights_ref[me] * packed[0].astype(jnp.float32)
    for d in range(1, n):
        exchange[d - 1].wait_recv()
        total = total + weights_ref[lax.rem(me - d + n, n)] * received[d].astype(jnp.float32)
    coadd = (total / jnp.full_like(total, weight_sum)).astype(jnp.bfloat16)
    templates_ref[0] = coadd
    library[me] = coadd

    spread = []
    for d in range(1, n):
        spread.append(
            pltpu.make_async_remote_copy(
                src_ref=library.at[me],
                dst_ref=library.at[me],
                send_sem=send2.at[d],
                recv_sem=recv2.at[d],
                device_id={"visit": lax.rem(me + d, n)},
                device_id_type=MESH,
            )
        )
        spread[-1].start()

    near = pl.multiple_of((1 - side) * (half - LANES), LANES)
    swap = []
    for d in range(n):
        source = lax.rem(me - d + n, n)
        if d:
            spread[d - 1].wait_recv()
        swap.append(
            pltpu.make_async_remote_copy(
                src_ref=library.at[source, :, pl.ds(near, LANES)],
                dst_ref=edges.at[source],
                send_sem=send3.at[d],
                recv_sem=recv3.at[d],
                device_id={"tile": 1 - side},
                device_id_type=MESH,
            )
        )
        swap[-1].start()
    for k in range(count):
        chosen[k * rows : (k + 1) * rows, 0:half] = library[slots[k]]
    for d in range(n):
        swap[d].wait_recv()
    for k in range(count):
        chosen[k * rows : (k + 1) * rows, half : half + LANES] = edges[slots[k]]

    for g in range(groups):
        tall = jnp.dot(
            row_band[...],
            chosen[g * LANES : (g + 1) * LANES, :],
            preferred_element_type=jnp.float32,
        ).astype(jnp.bfloat16)
        for b in range(basis):
            blurred[b, g * LANES : (g + 1) * LANES, :] = tall[b * LANES : (b + 1) * LANES, :]
    for g in range(groups):
        span = slice(g * LANES, (g + 1) * LANES)
        model = jnp.zeros((LANES, half), jnp.float32)
        for b in range(basis):
            smooth = jnp.dot(blurred[b, span, :], col_band[b], preferred_element_type=jnp.float32)
            model = model + factor[b, span, :] * smooth
        for k in range(group):
            model_ref[0, g * group + k] = model[k * rows : (k + 1) * rows, :]

    for copy in exchange + spread + swap:
        copy.wait_send()


def dense_body(science, warped, weights, coef, basis_rows, basis_cols, covered, owner):
    n = owner.shape[0]
    unused, count, rows, half = warped.shape
    basis = basis_rows.shape[0]
    vmem = pl.BlockSpec(memory_space=pltpu.VMEM)
    smem = pl.BlockSpec(memory_space=pltpu.SMEM)
    pixels = count * rows
    templates, model = pl.pallas_call(
        functools.partial(match_kernel, n),
        out_shape=(
            jax.ShapeDtypeStruct((1, rows, half), jnp.bfloat16),
            jax.ShapeDtypeStruct((1, count, rows, half), jnp.float32),
        ),
        in_specs=[pl.BlockSpec(memory_space=pl.ANY), vmem, vmem, vmem, smem, smem, smem],
        out_specs=(vmem, vmem),
        scratch_shapes=[
            pltpu.VMEM((count, rows, half), jnp.bfloat16),
            pltpu.VMEM((n, rows, half), jnp.bfloat16),
            pltpu.VMEM((n, rows, half), jnp.bfloat16),
            pltpu.VMEM((n, rows, half), jnp.bfloat16),
            pltpu.VMEM((n, rows, LANES), jnp.bfloat16),
            pltpu.VMEM((pixels, half + LANES), jnp.bfloat16),
            pltpu.VMEM((2, 16, LANES), jnp.float32),
            pltpu.VMEM((basis * LANES, LANES), jnp.bfloat16),
            pltpu.VMEM((basis, half + LANES, half), jnp.bfloat16),
            pltpu.VMEM((basis, pixels, half), jnp.float32),
            pltpu.VMEM((basis, pixels, half + LANES), jnp.bfloat16),
            pltpu.SemaphoreType.DMA,
        ]
        + [pltpu.SemaphoreType.DMA((n,))] * 6,
        compiler_params=pltpu.CompilerParams(
            collective_id=0, has_side_effects=True, vmem_limit_bytes=40 * 2**20
        ),
    )(warped, coef, basis_rows, basis_cols, weights, covered, owner)
    return templates, science.astype(jnp.float32) - model


def body(science, warped, weights, coef, basis_rows, basis_cols, covered, owner):
    tiles = owner.shape[0]
    dense = (
        covered.shape[1] == tiles
        and lax.axis_size("visit") == tiles
        and lax.axis_size("tile") == 2
    )
    chosen = dense_body if dense else sparse_body
    return chosen(science, warped, weights, coef, basis_rows, basis_cols, covered, owner)


def solution(mesh):
    in_specs = (
        P(("region", "visit"), None, None, "tile"),
        P(("region", "visit"), None, None, "tile"),
        P("region"),
        P(("region", "visit"), None, None, None),
        P(),
        P(),
        P("region", None),
        P("region"),
    )
    out_specs = (P(("region", "visit"), None, "tile"), P(("region", "visit"), None, None, "tile"))
    return jax.shard_map(body, mesh=mesh, in_specs=in_specs, out_specs=out_specs, check_vma=False)
```

```python
import functools

import jax
import jax.numpy as jnp
from jax import lax
from jax.experimental import pallas as pl
from jax.experimental.pallas import tpu as pltpu
from jax.sharding import PartitionSpec as P

MESH = pl.DeviceIdType.MESH
LANES = 128


def padded(block, sides, width):
    for axis, dim in sides:
        count = lax.axis_size(axis)
        forward = [(i, i + 1) for i in range(count - 1)]
        backward = [(target, source) for source, target in forward]
        low = lax.ppermute(
            lax.slice_in_dim(block, block.shape[dim] - width, None, axis=dim), axis, forward
        )
        high = lax.ppermute(lax.slice_in_dim(block, 0, width, axis=dim), axis, backward)
        block = jnp.concatenate([low, block, high], axis=dim)
    return block


def polynomials(rows, half, offset, total):
    yn = (2.0 * jnp.arange(rows, dtype=jnp.float32) + 1.0) / rows - 1.0
    columns = (offset + lax.iota(jnp.int32, half)).astype(jnp.float32)
    xn = (2.0 * columns + 1.0) / total - 1.0
    ygrid = jnp.broadcast_to(yn[:, None], (rows, half))
    xgrid = jnp.broadcast_to(xn[None, :], (rows, half))
    ones = jnp.ones((rows, half), jnp.float32)
    return jnp.stack([ones, xgrid, ygrid, xgrid * xgrid, xgrid * ygrid, ygrid * ygrid])


def band_matrix(profile, offsets):
    band = jnp.zeros((profile.shape[0],) + offsets.shape, jnp.bfloat16)
    for i in range(profile.shape[1]):
        band = jnp.where((offsets == i)[None], profile[:, i][:, None, None], band)
    return band


def sparse_body(science, warped, weights, coef, basis_rows, basis_cols, covered, owner):
    count, rows, half = (warped.shape[1], warped.shape[2], warped.shape[3])
    tiles = owner.shape[0]
    visit_count = lax.axis_size("visit")
    visit_here = lax.axis_index("visit")
    side_here = lax.axis_index("tile")
    side_count = lax.axis_size("tile")
    tile_dev = tiles // visit_count
    ksize = basis_rows.shape[1]
    reach = ksize // 2
    width = half + 2 * reach
    wanted = lax.iota(jnp.int32, tiles)
    slots = jnp.take(owner, covered)
    slot_of = lax.dynamic_slice_in_dim(slots, visit_here, 1, 0)[0]
    hits = (slots[:, :, None] == wanted).astype(jnp.float32)
    slot_weight = jnp.sum(weights[:, None, None] * hits, axis=(0, 1))
    flat_pixels = warped[0].reshape(count, rows * half)
    select = (slot_of[None, :] == wanted[:, None]).astype(jnp.bfloat16)
    packed = jnp.dot(select, flat_pixels, preferred_element_type=jnp.float32).astype(jnp.bfloat16)
    received = lax.all_to_all(packed, "visit", split_axis=0, concat_axis=0, tiled=True)
    received = received.reshape(visit_count, tile_dev, rows * half)
    total = jnp.sum(weights[:, None, None] * received.astype(jnp.float32), axis=0)
    mine_weight = lax.dynamic_slice_in_dim(slot_weight, visit_here * tile_dev, tile_dev, 0)
    templates = (total / mine_weight[:, None]).astype(jnp.bfloat16).reshape(tile_dev, rows, half)
    library = lax.all_gather(templates, "visit", axis=0, tiled=True)
    picks = jnp.dot(
        select.T, library.reshape(tiles, rows * half), preferred_element_type=jnp.float32
    )
    chosen = picks.astype(jnp.bfloat16).reshape(count, rows, half)
    chosen = padded(chosen, (("tile", 2),), reach)
    row_offsets = lax.iota(jnp.int32, rows)[None, :] - lax.iota(jnp.int32, rows)[:, None] + reach
    row_band = band_matrix(basis_rows, row_offsets)
    col_offsets = lax.iota(jnp.int32, width)[:, None] - lax.iota(jnp.int32, half)[None, :]
    col_band = band_matrix(basis_cols, col_offsets)
    polys = polynomials(rows, half, side_here * half, half * side_count)
    pairs = count // 2
    tpl_blocks = chosen.reshape(pairs, 2, rows, width)
    sci_blocks = science[0].reshape(pairs, 2, rows, half)
    coef_blocks = coef[0].reshape(pairs, 2, coef.shape[2], coef.shape[3])

    def match(item):
        tpl, sci, cf = item
        blurred = jnp.einsum(
            "byz,kzx->kbyx", row_band, tpl, preferred_element_type=jnp.float32
        ).astype(jnp.bfloat16)
        smooth = jnp.einsum("kbyx,bxw->kbyw", blurred, col_band, preferred_element_type=jnp.float32)
        factor = jnp.einsum("kbp,pyw->kbyw", cf, polys, precision=lax.Precision.HIGHEST)
        return sci.astype(jnp.float32) - jnp.sum(factor * smooth, axis=1)

    difference = lax.map(match, (tpl_blocks, sci_blocks, coef_blocks)).reshape(1, count, rows, half)
    return (templates, difference)


def match_kernel(
    n,
    warped_hbm,
    coef_hbm,
    rows_hbm,
    cols_hbm,
    weights_hbm,
    covered_hbm,
    owner_hbm,
    templates_ref,
    model_ref,
    warped,
    coef_ref,
    rows_ref,
    cols_ref,
    weights_ref,
    covered_ref,
    owner_ref,
    packed,
    received,
    library,
    edges,
    chosen,
    profiles,
    row_band,
    col_band,
    factor,
    blurred,
    load_sem,
    send1,
    recv1,
    send2,
    recv2,
    send3,
    recv3,
):
    count, rows, half = warped.shape
    basis, ksize = rows_ref.shape
    reach = ksize // 2
    me = lax.axis_index("visit")
    side = lax.axis_index("tile")
    group = LANES // rows
    groups = count // group

    def partner(d):
        x, z = me % 2, me // 2
        across = d % 2
        over = [d // 2 // 2**bit % 2 for bit in range(8)]
        there = 0
        for bit in range(8):
            digit = z // 2**bit % 2
            there = there + 2**bit * (1 - digit if over[bit] else digit)
        return 2 * there + (1 - x if across else x)

    order = list(range(n - 1, 0, -1))
    barrier = pltpu.get_barrier_semaphore()
    for d in order:
        pl.semaphore_signal(
            barrier, inc=1, device_id={"visit": partner(d)}, device_id_type=MESH
        )
    pl.semaphore_signal(barrier, inc=1, device_id={"tile": 1 - side}, device_id_type=MESH)

    loads = [
        pltpu.make_async_copy(source, target, load_sem.at[i])
        for i, (source, target) in enumerate(
            (
                (covered_hbm, covered_ref),
                (owner_hbm, owner_ref),
                (warped_hbm.at[0], warped),
                (weights_hbm, weights_ref),
                (rows_hbm, rows_ref),
                (cols_hbm, cols_ref),
                (coef_hbm, coef_ref),
            )
        )
    ]
    for load in loads:
        load.start()
    for load in loads[:3]:
        load.wait()
    slots = [owner_ref[covered_ref[me, k]] for k in range(count)]
    for d in range(n):
        target = partner(d)
        k_of = jnp.int32(0)
        for k in range(1, count):
            k_of = jnp.where(slots[k] == target, jnp.int32(k), k_of)
        packed[d] = warped[k_of]
    pl.semaphore_wait(barrier, n)

    exchange = []
    for d in order:
        exchange.append(
            pltpu.make_async_remote_copy(
                src_ref=packed.at[d],
                dst_ref=received.at[d],
                send_sem=send1.at[d],
                recv_sem=recv1.at[d],
                device_id={"visit": partner(d)},
                device_id_type=MESH,
            )
        )
        exchange[-1].start()

    for load in loads[3:]:
        load.wait()
    profiles[...] = jnp.zeros_like(profiles)
    profiles[0, 0:basis, 0:ksize] = rows_ref[...].astype(jnp.float32)
    profiles[1, 0:basis, 0:ksize] = cols_ref[...].astype(jnp.float32)
    zi = lax.broadcasted_iota(jnp.int32, (LANES, LANES), 0)
    xi = lax.broadcasted_iota(jnp.int32, (LANES, LANES), 1)
    flip = (zi + xi == ksize - 1).astype(jnp.bfloat16)
    profiles[1] = jnp.dot(
        profiles[1].astype(jnp.bfloat16), flip, preferred_element_type=jnp.float32
    )
    same = (zi // rows) == (xi // rows)
    centre = jnp.abs(zi - xi) <= reach
    above = zi - xi > LANES // 2
    below = xi - zi > LANES // 2
    zero = jnp.zeros((LANES, LANES), jnp.float32)

    def circulant(which, b):
        line = jnp.broadcast_to(profiles[which, b : b + 1, :], (LANES, LANES))
        return pltpu.roll(line, LANES - reach, 1, stride=1, stride_axis=0)

    for b in range(basis):
        row_band[b * LANES : (b + 1) * LANES, :] = jnp.where(same, circulant(0, b), zero).astype(
            jnp.bfloat16
        )
        ring = circulant(1, b)
        diagonal = jnp.where(centre, ring, zero).astype(jnp.bfloat16)
        upper = jnp.where(above, ring, zero)
        lower = jnp.where(below, ring, zero)
        for j in range(half // LANES):
            for i in range(half // LANES):
                block = (
                    diagonal
                    if i == j
                    else upper.astype(jnp.bfloat16)
                    if i == j - 1
                    else lower.astype(jnp.bfloat16)
                    if i == j + 1
                    else zero.astype(jnp.bfloat16)
                )
                col_band[b, i * LANES : (i + 1) * LANES, j * LANES : (j + 1) * LANES] = block
            edge = zero
            if j == half // LANES - 1:
                edge = jnp.where(side == 0, lower, edge)
            if j == 0:
                edge = jnp.where(side == 1, upper, edge)
            col_band[b, half : half + LANES, j * LANES : (j + 1) * LANES] = edge.astype(
                jnp.bfloat16
            )

    line = lax.broadcasted_iota(jnp.int32, (rows, 1), 0)
    yn = (2.0 * line.astype(jnp.float32) + 1.0) / rows - 1.0
    column = lax.broadcasted_iota(jnp.int32, (rows, half), 1) + side * half
    xn = (2.0 * column.astype(jnp.float32) + 1.0) / (2 * half) - 1.0

    def factors(k, carry):
        c = [coef_ref[0, p, pl.ds(k, 1), :] for p in range(coef_ref.shape[1])]
        constant = c[0] + yn * (c[2] + yn * c[5])
        linear = c[1] + yn * c[4]
        square = c[3]
        start = pl.multiple_of(k * rows, rows)
        for b in range(basis):
            p0, p1, p2 = (p[:, b : b + 1] for p in (constant, linear, square))
            factor[b, pl.ds(start, rows), :] = p0 + xn * (p1 + xn * p2)
        return carry

    lax.fori_loop(0, count, factors, 0)

    weight_sum = weights_ref[0]
    for v in range(1, n):
        weight_sum = weight_sum + weights_ref[v]
    total = weights_ref[me] * packed[0].astype(jnp.float32)
    for d in range(1, n):
        exchange[order.index(d)].wait_recv()
        total = total + weights_ref[partner(d)] * received[d].astype(jnp.float32)
    coadd = (total / jnp.full_like(total, weight_sum)).astype(jnp.bfloat16)
    library[me] = coadd

    spread = []
    for d in order:
        spread.append(
            pltpu.make_async_remote_copy(
                src_ref=library.at[me],
                dst_ref=library.at[me],
                send_sem=send2.at[d],
                recv_sem=recv2.at[d],
                device_id={"visit": partner(d)},
                device_id_type=MESH,
            )
        )
        spread[-1].start()

    templates_ref[0] = coadd
    near = pl.multiple_of((1 - side) * (half - LANES), LANES)
    swap = []
    for d in range(n):
        source = partner(d)
        if d:
            spread[order.index(d)].wait_recv()
        swap.append(
            pltpu.make_async_remote_copy(
                src_ref=library.at[source, :, pl.ds(near, LANES)],
                dst_ref=edges.at[source],
                send_sem=send3.at[d],
                recv_sem=recv3.at[d],
                device_id={"tile": 1 - side},
                device_id_type=MESH,
            )
        )
        swap[-1].start()
    for k in range(count):
        chosen[k * rows : (k + 1) * rows, 0:half] = library[slots[k]]
    for d in range(n):
        swap[d].wait_recv()
    for k in range(count):
        chosen[k * rows : (k + 1) * rows, half : half + LANES] = edges[slots[k]]

    for g in range(groups):
        tall = jnp.dot(
            row_band[...],
            chosen[g * LANES : (g + 1) * LANES, :],
            preferred_element_type=jnp.float32,
        ).astype(jnp.bfloat16)
        for b in range(basis):
            blurred[b, g * LANES : (g + 1) * LANES, :] = tall[b * LANES : (b + 1) * LANES, :]
    for g in range(groups):
        span = slice(g * LANES, (g + 1) * LANES)
        model = jnp.zeros((LANES, half), jnp.float32)
        for b in range(basis):
            smooth = jnp.dot(blurred[b, span, :], col_band[b], preferred_element_type=jnp.float32)
            model = model + factor[b, span, :] * smooth
        for k in range(group):
            model_ref[0, g * group + k] = model[k * rows : (k + 1) * rows, :]

    for copy in exchange + spread + swap:
        copy.wait_send()


def dense_body(science, warped, weights, coef, basis_rows, basis_cols, covered, owner):
    n = owner.shape[0]
    unused, count, rows, half = warped.shape
    basis = basis_rows.shape[0]
    vmem = pl.BlockSpec(memory_space=pltpu.VMEM)
    pixels = count * rows
    templates, model = pl.pallas_call(
        functools.partial(match_kernel, n),
        out_shape=(
            jax.ShapeDtypeStruct((1, rows, half), jnp.bfloat16),
            jax.ShapeDtypeStruct((1, count, rows, half), jnp.float32),
        ),
        in_specs=[pl.BlockSpec(memory_space=pl.ANY)] * 7,
        out_specs=(vmem, vmem),
        scratch_shapes=[
            pltpu.VMEM((count, rows, half), jnp.bfloat16),
            pltpu.VMEM((1, coef.shape[3], count, basis), jnp.float32),
            pltpu.VMEM(basis_rows.shape, jnp.bfloat16),
            pltpu.VMEM(basis_cols.shape, jnp.bfloat16),
            pltpu.SMEM(weights.shape, jnp.float32),
            pltpu.SMEM(covered.shape, jnp.int32),
            pltpu.SMEM(owner.shape, jnp.int32),
            pltpu.VMEM((n, rows, half), jnp.bfloat16),
            pltpu.VMEM((n, rows, half), jnp.bfloat16),
            pltpu.VMEM((n, rows, half), jnp.bfloat16),
            pltpu.VMEM((n, rows, LANES), jnp.bfloat16),
            pltpu.VMEM((pixels, half + LANES), jnp.bfloat16),
            pltpu.VMEM((2, 16, LANES), jnp.float32),
            pltpu.VMEM((basis * LANES, LANES), jnp.bfloat16),
            pltpu.VMEM((basis, half + LANES, half), jnp.bfloat16),
            pltpu.VMEM((basis, pixels, half), jnp.float32),
            pltpu.VMEM((basis, pixels, half + LANES), jnp.bfloat16),
            pltpu.SemaphoreType.DMA((7,)),
        ]
        + [pltpu.SemaphoreType.DMA((n,))] * 6,
        compiler_params=pltpu.CompilerParams(
            collective_id=0, has_side_effects=True, vmem_limit_bytes=40 * 2**20
        ),
    )(
        *(
            pltpu.with_memory_space_constraint(operand, pltpu.HBM)
            for operand in (
                warped,
                jnp.transpose(coef, (0, 3, 1, 2)),
                basis_rows,
                basis_cols,
                weights,
                covered,
                owner,
            )
        )
    )
    return templates, science.astype(jnp.float32) - model


def body(science, warped, weights, coef, basis_rows, basis_cols, covered, owner):
    tiles = owner.shape[0]
    dense = (
        covered.shape[1] == tiles
        and lax.axis_size("visit") == tiles
        and lax.axis_size("tile") == 2
    )
    chosen = dense_body if dense else sparse_body
    return chosen(science, warped, weights, coef, basis_rows, basis_cols, covered, owner)


def solution(mesh):
    in_specs = (
        P(("region", "visit"), None, None, "tile"),
        P(("region", "visit"), None, None, "tile"),
        P("region"),
        P(("region", "visit"), None, None, None),
        P(),
        P(),
        P("region", None),
        P("region"),
    )
    out_specs = (P(("region", "visit"), None, "tile"), P(("region", "visit"), None, None, "tile"))
    return jax.shard_map(body, mesh=mesh, in_specs=in_specs, out_specs=out_specs, check_vma=False)
```

```python
import functools

import jax
import jax.numpy as jnp
from jax import lax
from jax.experimental import pallas as pl
from jax.experimental.pallas import tpu as pltpu
from jax.sharding import PartitionSpec as P

MESH = pl.DeviceIdType.MESH
LANES = 128


def padded(block, sides, width):
    for axis, dim in sides:
        count = lax.axis_size(axis)
        forward = [(i, i + 1) for i in range(count - 1)]
        backward = [(target, source) for source, target in forward]
        low = lax.ppermute(
            lax.slice_in_dim(block, block.shape[dim] - width, None, axis=dim), axis, forward
        )
        high = lax.ppermute(lax.slice_in_dim(block, 0, width, axis=dim), axis, backward)
        block = jnp.concatenate([low, block, high], axis=dim)
    return block


def polynomials(rows, half, offset, total):
    yn = (2.0 * jnp.arange(rows, dtype=jnp.float32) + 1.0) / rows - 1.0
    columns = (offset + lax.iota(jnp.int32, half)).astype(jnp.float32)
    xn = (2.0 * columns + 1.0) / total - 1.0
    ygrid = jnp.broadcast_to(yn[:, None], (rows, half))
    xgrid = jnp.broadcast_to(xn[None, :], (rows, half))
    ones = jnp.ones((rows, half), jnp.float32)
    return jnp.stack([ones, xgrid, ygrid, xgrid * xgrid, xgrid * ygrid, ygrid * ygrid])


def band_matrix(profile, offsets):
    band = jnp.zeros((profile.shape[0],) + offsets.shape, jnp.bfloat16)
    for i in range(profile.shape[1]):
        band = jnp.where((offsets == i)[None], profile[:, i][:, None, None], band)
    return band


def sparse_body(science, warped, weights, coef, basis_rows, basis_cols, covered, owner):
    count, rows, half = (warped.shape[1], warped.shape[2], warped.shape[3])
    tiles = owner.shape[0]
    visit_count = lax.axis_size("visit")
    visit_here = lax.axis_index("visit")
    side_here = lax.axis_index("tile")
    side_count = lax.axis_size("tile")
    tile_dev = tiles // visit_count
    ksize = basis_rows.shape[1]
    reach = ksize // 2
    width = half + 2 * reach
    wanted = lax.iota(jnp.int32, tiles)
    slots = jnp.take(owner, covered)
    slot_of = lax.dynamic_slice_in_dim(slots, visit_here, 1, 0)[0]
    hits = (slots[:, :, None] == wanted).astype(jnp.float32)
    slot_weight = jnp.sum(weights[:, None, None] * hits, axis=(0, 1))
    flat_pixels = warped[0].reshape(count, rows * half)
    select = (slot_of[None, :] == wanted[:, None]).astype(jnp.bfloat16)
    packed = jnp.dot(select, flat_pixels, preferred_element_type=jnp.float32).astype(jnp.bfloat16)
    received = lax.all_to_all(packed, "visit", split_axis=0, concat_axis=0, tiled=True)
    received = received.reshape(visit_count, tile_dev, rows * half)
    total = jnp.sum(weights[:, None, None] * received.astype(jnp.float32), axis=0)
    mine_weight = lax.dynamic_slice_in_dim(slot_weight, visit_here * tile_dev, tile_dev, 0)
    templates = (total / mine_weight[:, None]).astype(jnp.bfloat16).reshape(tile_dev, rows, half)
    library = lax.all_gather(templates, "visit", axis=0, tiled=True)
    picks = jnp.dot(
        select.T, library.reshape(tiles, rows * half), preferred_element_type=jnp.float32
    )
    chosen = picks.astype(jnp.bfloat16).reshape(count, rows, half)
    chosen = padded(chosen, (("tile", 2),), reach)
    row_offsets = lax.iota(jnp.int32, rows)[None, :] - lax.iota(jnp.int32, rows)[:, None] + reach
    row_band = band_matrix(basis_rows, row_offsets)
    col_offsets = lax.iota(jnp.int32, width)[:, None] - lax.iota(jnp.int32, half)[None, :]
    col_band = band_matrix(basis_cols, col_offsets)
    polys = polynomials(rows, half, side_here * half, half * side_count)
    pairs = count // 2
    tpl_blocks = chosen.reshape(pairs, 2, rows, width)
    sci_blocks = science[0].reshape(pairs, 2, rows, half)
    coef_blocks = coef[0].reshape(pairs, 2, coef.shape[2], coef.shape[3])

    def match(item):
        tpl, sci, cf = item
        blurred = jnp.einsum(
            "byz,kzx->kbyx", row_band, tpl, preferred_element_type=jnp.float32
        ).astype(jnp.bfloat16)
        smooth = jnp.einsum("kbyx,bxw->kbyw", blurred, col_band, preferred_element_type=jnp.float32)
        factor = jnp.einsum("kbp,pyw->kbyw", cf, polys, precision=lax.Precision.HIGHEST)
        return sci.astype(jnp.float32) - jnp.sum(factor * smooth, axis=1)

    difference = lax.map(match, (tpl_blocks, sci_blocks, coef_blocks)).reshape(1, count, rows, half)
    return (templates, difference)


def match_kernel(
    n,
    warped_hbm,
    coef_hbm,
    rows_hbm,
    cols_hbm,
    weights_hbm,
    covered_hbm,
    owner_hbm,
    templates_ref,
    model_ref,
    warped,
    coef_ref,
    rows_ref,
    cols_ref,
    weights_ref,
    covered_ref,
    owner_ref,
    packed,
    received,
    library,
    edges,
    chosen,
    profiles,
    row_band,
    col_band,
    factor,
    blurred,
    load_sem,
    send1,
    recv1,
    send2,
    recv2,
    send3,
    recv3,
):
    count, rows, half = warped.shape
    basis, ksize = rows_ref.shape
    reach = ksize // 2
    me = lax.axis_index("visit")
    side = lax.axis_index("tile")
    group = LANES // rows
    groups = count // group

    def partner(d):
        x, z = me % 2, me // 2
        across = d % 2
        over = [d // 2 // 2**bit % 2 for bit in range(8)]
        there = 0
        for bit in range(8):
            digit = z // 2**bit % 2
            there = there + 2**bit * (1 - digit if over[bit] else digit)
        return 2 * there + (1 - x if across else x)

    order = list(range(n - 1, 0, -1))
    barrier = pltpu.get_barrier_semaphore()
    for d in order:
        pl.semaphore_signal(
            barrier, inc=1, device_id={"visit": partner(d)}, device_id_type=MESH
        )
    pl.semaphore_signal(barrier, inc=1, device_id={"tile": 1 - side}, device_id_type=MESH)

    loads = [
        pltpu.make_async_copy(source, target, load_sem.at[i])
        for i, (source, target) in enumerate(
            (
                (covered_hbm, covered_ref),
                (owner_hbm, owner_ref),
                (warped_hbm.at[0], warped),
                (weights_hbm, weights_ref),
                (rows_hbm, rows_ref),
                (cols_hbm, cols_ref),
                (coef_hbm, coef_ref),
            )
        )
    ]
    for load in loads:
        load.start()
    for load in loads[:3]:
        load.wait()
    slots = [owner_ref[covered_ref[me, k]] for k in range(count)]
    for d in range(n):
        target = partner(d)
        k_of = jnp.int32(0)
        for k in range(1, count):
            k_of = jnp.where(slots[k] == target, jnp.int32(k), k_of)
        packed[d] = warped[k_of]
    pl.semaphore_wait(barrier, n)

    exchange = []
    for d in order:
        exchange.append(
            pltpu.make_async_remote_copy(
                src_ref=packed.at[d],
                dst_ref=received.at[d],
                send_sem=send1.at[d],
                recv_sem=recv1.at[d],
                device_id={"visit": partner(d)},
                device_id_type=MESH,
            )
        )
        exchange[-1].start()

    for load in loads[3:]:
        load.wait()
    profiles[...] = jnp.zeros_like(profiles)
    profiles[0, 0:basis, 0:ksize] = rows_ref[...].astype(jnp.float32)
    profiles[1, 0:basis, 0:ksize] = cols_ref[...].astype(jnp.float32)
    zi = lax.broadcasted_iota(jnp.int32, (LANES, LANES), 0)
    xi = lax.broadcasted_iota(jnp.int32, (LANES, LANES), 1)
    flip = (zi + xi == ksize - 1).astype(jnp.bfloat16)
    profiles[1] = jnp.dot(
        profiles[1].astype(jnp.bfloat16), flip, preferred_element_type=jnp.float32
    )
    same = (zi // rows) == (xi // rows)
    centre = jnp.abs(zi - xi) <= reach
    above = zi - xi > LANES // 2
    below = xi - zi > LANES // 2
    zero = jnp.zeros((LANES, LANES), jnp.float32)

    def circulant(which, b):
        line = jnp.broadcast_to(profiles[which, b : b + 1, :], (LANES, LANES))
        return pltpu.roll(line, LANES - reach, 1, stride=1, stride_axis=0)

    for b in range(basis):
        row_band[b * LANES : (b + 1) * LANES, :] = jnp.where(same, circulant(0, b), zero).astype(
            jnp.bfloat16
        )
        ring = circulant(1, b)
        diagonal = jnp.where(centre, ring, zero).astype(jnp.bfloat16)
        upper = jnp.where(above, ring, zero)
        lower = jnp.where(below, ring, zero)
        for j in range(half // LANES):
            for i in range(half // LANES):
                block = (
                    diagonal
                    if i == j
                    else upper.astype(jnp.bfloat16)
                    if i == j - 1
                    else lower.astype(jnp.bfloat16)
                    if i == j + 1
                    else zero.astype(jnp.bfloat16)
                )
                col_band[b, i * LANES : (i + 1) * LANES, j * LANES : (j + 1) * LANES] = block
            edge = zero
            if j == half // LANES - 1:
                edge = jnp.where(side == 0, lower, edge)
            if j == 0:
                edge = jnp.where(side == 1, upper, edge)
            col_band[b, half : half + LANES, j * LANES : (j + 1) * LANES] = edge.astype(
                jnp.bfloat16
            )

    line = lax.broadcasted_iota(jnp.int32, (rows, 1), 0)
    yn = (2.0 * line.astype(jnp.float32) + 1.0) / rows - 1.0
    column = lax.broadcasted_iota(jnp.int32, (rows, half), 1) + side * half
    xn = (2.0 * column.astype(jnp.float32) + 1.0) / (2 * half) - 1.0

    def factors(k, carry):
        c = [coef_ref[0, p, pl.ds(k, 1), :] for p in range(coef_ref.shape[1])]
        constant = c[0] + yn * (c[2] + yn * c[5])
        linear = c[1] + yn * c[4]
        square = c[3]
        start = pl.multiple_of(k * rows, rows)
        for b in range(basis):
            p0, p1, p2 = (p[:, b : b + 1] for p in (constant, linear, square))
            factor[b, pl.ds(start, rows), :] = p0 + xn * (p1 + xn * p2)
        return carry

    lax.fori_loop(0, count, factors, 0)

    weight_sum = weights_ref[0]
    for v in range(1, n):
        weight_sum = weight_sum + weights_ref[v]
    total = weights_ref[me] * packed[0].astype(jnp.float32)
    for d in range(1, n):
        exchange[order.index(d)].wait_recv()
        total = total + weights_ref[partner(d)] * received[d].astype(jnp.float32)
    coadd = (total / jnp.full_like(total, weight_sum)).astype(jnp.bfloat16)
    library[me] = coadd

    spread = []
    for d in order:
        spread.append(
            pltpu.make_async_remote_copy(
                src_ref=library.at[me],
                dst_ref=library.at[me],
                send_sem=send2.at[d],
                recv_sem=recv2.at[d],
                device_id={"visit": partner(d)},
                device_id_type=MESH,
            )
        )
        spread[-1].start()

    templates_ref[0] = coadd
    near = pl.multiple_of((1 - side) * (half - LANES), LANES)
    swap = []
    for d in range(n):
        source = partner(d)
        if d:
            spread[order.index(d)].wait_recv()
        swap.append(
            pltpu.make_async_remote_copy(
                src_ref=library.at[source, :, pl.ds(near, LANES)],
                dst_ref=edges.at[source],
                send_sem=send3.at[d],
                recv_sem=recv3.at[d],
                device_id={"tile": 1 - side},
                device_id_type=MESH,
            )
        )
        swap[-1].start()
    for k in range(count):
        chosen[k * rows : (k + 1) * rows, 0:half] = library[slots[k]]

    def blur(columns):
        for g in range(groups):
            tall = jnp.dot(
                row_band[...],
                chosen[g * LANES : (g + 1) * LANES, columns],
                preferred_element_type=jnp.float32,
            ).astype(jnp.bfloat16)
            for b in range(basis):
                blurred[b, g * LANES : (g + 1) * LANES, columns] = tall[
                    b * LANES : (b + 1) * LANES, :
                ]

    blur(slice(0, half))
    for d in range(n):
        swap[d].wait_recv()
    for k in range(count):
        chosen[k * rows : (k + 1) * rows, half : half + LANES] = edges[slots[k]]
    blur(slice(half, half + LANES))
    for g in range(groups):
        span = slice(g * LANES, (g + 1) * LANES)
        model = jnp.zeros((LANES, half), jnp.float32)
        for b in range(basis):
            smooth = jnp.dot(blurred[b, span, :], col_band[b], preferred_element_type=jnp.float32)
            model = model + factor[b, span, :] * smooth
        for k in range(group):
            model_ref[0, g * group + k] = model[k * rows : (k + 1) * rows, :]

    for copy in exchange + spread + swap:
        copy.wait_send()


def dense_body(science, warped, weights, coef, basis_rows, basis_cols, covered, owner):
    n = owner.shape[0]
    unused, count, rows, half = warped.shape
    basis = basis_rows.shape[0]
    vmem = pl.BlockSpec(memory_space=pltpu.VMEM)
    pixels = count * rows
    templates, model = pl.pallas_call(
        functools.partial(match_kernel, n),
        out_shape=(
            jax.ShapeDtypeStruct((1, rows, half), jnp.bfloat16),
            jax.ShapeDtypeStruct((1, count, rows, half), jnp.float32),
        ),
        in_specs=[pl.BlockSpec(memory_space=pl.ANY)] * 7,
        out_specs=(vmem, vmem),
        scratch_shapes=[
            pltpu.VMEM((count, rows, half), jnp.bfloat16),
            pltpu.VMEM((1, coef.shape[3], count, basis), jnp.float32),
            pltpu.VMEM(basis_rows.shape, jnp.bfloat16),
            pltpu.VMEM(basis_cols.shape, jnp.bfloat16),
            pltpu.SMEM(weights.shape, jnp.float32),
            pltpu.SMEM(covered.shape, jnp.int32),
            pltpu.SMEM(owner.shape, jnp.int32),
            pltpu.VMEM((n, rows, half), jnp.bfloat16),
            pltpu.VMEM((n, rows, half), jnp.bfloat16),
            pltpu.VMEM((n, rows, half), jnp.bfloat16),
            pltpu.VMEM((n, rows, LANES), jnp.bfloat16),
            pltpu.VMEM((pixels, half + LANES), jnp.bfloat16),
            pltpu.VMEM((2, 16, LANES), jnp.float32),
            pltpu.VMEM((basis * LANES, LANES), jnp.bfloat16),
            pltpu.VMEM((basis, half + LANES, half), jnp.bfloat16),
            pltpu.VMEM((basis, pixels, half), jnp.float32),
            pltpu.VMEM((basis, pixels, half + LANES), jnp.bfloat16),
            pltpu.SemaphoreType.DMA((7,)),
        ]
        + [pltpu.SemaphoreType.DMA((n,))] * 6,
        compiler_params=pltpu.CompilerParams(
            collective_id=0, has_side_effects=True, vmem_limit_bytes=40 * 2**20
        ),
    )(
        *(
            pltpu.with_memory_space_constraint(operand, pltpu.HBM)
            for operand in (
                warped,
                jnp.transpose(coef, (0, 3, 1, 2)),
                basis_rows,
                basis_cols,
                weights,
                covered,
                owner,
            )
        )
    )
    return templates, science.astype(jnp.float32) - model


def body(science, warped, weights, coef, basis_rows, basis_cols, covered, owner):
    tiles = owner.shape[0]
    dense = (
        covered.shape[1] == tiles
        and lax.axis_size("visit") == tiles
        and lax.axis_size("tile") == 2
    )
    chosen = dense_body if dense else sparse_body
    return chosen(science, warped, weights, coef, basis_rows, basis_cols, covered, owner)


def solution(mesh):
    in_specs = (
        P(("region", "visit"), None, None, "tile"),
        P(("region", "visit"), None, None, "tile"),
        P("region"),
        P(("region", "visit"), None, None, None),
        P(),
        P(),
        P("region", None),
        P("region"),
    )
    out_specs = (P(("region", "visit"), None, "tile"), P(("region", "visit"), None, None, "tile"))
    return jax.shard_map(body, mesh=mesh, in_specs=in_specs, out_specs=out_specs, check_vma=False)
```
